256 devices in a mesh: dp: 32 (over z_lo, y, core), tensor: 8 (over x, z_hi).
Axes of the slice: x: 4, y: 4, z: 8 (z_hi: 2, z_lo: 4; z = z_hi * 4 + z_lo), core: 2. Of those that a mesh axis runs over, the one named last changes fastest.
Arguments:
- grad: bfloat16 [32, 1024, 16384], P('dp', None, 'tensor'), may hold values from -6 to 6
- error: bfloat16 [32, 1024, 16384], P('dp', None, 'tensor'), may hold values from -4 to 4
- q_init: bfloat16 [16384, 32], P('tensor'), may hold values from -6 to 6
Outputs:
- p_basis: float32 [1024, 32], P(('dp', 'tensor'))
- q_factor: float32 [16384, 32], P('tensor')
- new_error: bfloat16 [32, 1024, 16384], P('dp', None, 'tensor')
The draws below stay inside these ranges and needn't reach their ends.
All inputs are finite; a program needn't handle non-finite values.
Results may differ from the reference program's by a relative error of at most 0.03.
Values may be sent and summed in bfloat16 or wider, within the bound.
No kernel may reach another device: no remote copies, remote signals or barrier semaphores. Data moves between devices by JAX's collectives and lax.ppermute only.
A program may use at most 64 MiB of HBM per device.

```python
import math
import jax
import jax.numpy as jnp
from jax import lax

ROWS = 1024
RANK = 32
ITERS = 3
COLS = 16384
N_DP = 32


def level_of(key, dims, cuts, least, top_value):
    def one(position, parts):
        heights = jax.random.uniform(jax.random.fold_in(jax.random.fold_in(key, 6), position), (parts,), jnp.float32, least / len(cuts), top_value / len(cuts))
        return jnp.repeat(jnp.exp(heights), dims[position] // parts).reshape((-1,) + (1,) * (len(dims) - position - 1))

    loudness = one(*cuts[0])
    for cut in cuts[1:]:
        loudness = loudness * one(*cut)
    return loudness


def noise(stream_key, shape, spread, most, cuts=(), kind=jnp.bfloat16):
    loudness = level_of(stream_key, shape, cuts, -0.22, 0.18) if cuts else 1.0
    array = jax.random.normal(stream_key, shape, jnp.float32) * spread * loudness
    return jnp.minimum(jnp.maximum(array, -most), most).astype(kind)


def setup_inputs(seed: int = 0) -> dict:
    seeds = jax.random.split(jax.random.key(seed), 4)
    return {
        "grad": noise(seeds[0], (N_DP, ROWS, COLS), 1.0, 6.0, ((0, 32), (2, 8))),
        "error": noise(seeds[1], (N_DP, ROWS, COLS), 0.5, 4.0, ((0, 32), (2, 8))),
        "q_init": noise(seeds[2], (COLS, RANK), 1.0, 6.0, ((0, 8),)),
    }


def orthonormal(left):
    gram = jnp.dot(left.T, left, precision=lax.Precision.HIGHEST)
    chol = jnp.linalg.cholesky(gram)
    return lax.linalg.triangular_solve(chol, left, left_side=False, lower=True, transpose_a=True)

def reference(grad, error, q_init):
    corrected = (grad.astype(jnp.float32) + error.astype(jnp.float32)).astype(jnp.bfloat16)
    qb = q_init
    basis = jnp.zeros((ROWS, RANK), jnp.float32)
    right = jnp.zeros((COLS, RANK), jnp.float32)
    pb = basis.astype(jnp.bfloat16)
    for step in range(ITERS):

        def left_term(block):
            return jnp.dot(block.astype(jnp.float32), qb.astype(jnp.float32), preferred_element_type=jnp.float32)
        left = lax.optimization_barrier(jnp.sum(lax.map(left_term, corrected), axis=0)) / N_DP
        basis = orthonormal(left)
        pb = basis.astype(jnp.bfloat16)

        def right_term(block):
            return jnp.dot(block.T.astype(jnp.float32), pb.astype(jnp.float32), preferred_element_type=jnp.float32)
        right = lax.optimization_barrier(jnp.sum(lax.map(right_term, corrected), axis=0)) / N_DP
        qb = right.astype(jnp.bfloat16)
    approx = jnp.dot(pb.astype(jnp.float32), qb.T.astype(jnp.float32), preferred_element_type=jnp.float32)
    new_error = (corrected.astype(jnp.float32) - approx[None]).astype(jnp.bfloat16)
    return (basis * math.sqrt(ROWS), right / math.sqrt(ROWS), new_error)
```

```python
import math

import jax
import jax.numpy as jnp
from jax import lax
from jax.sharding import Mesh, PartitionSpec as P

ROWS = 1024
ITERS = 3
SWAP = [(0, 1), (1, 0)]
CHIPS = ("zl", "y", "x", "zh")


def shift(n, d):
    return [(i, (i + d) % n) for i in range(n)]


def exchange_sum(value, axis, width):
    n = lax.axis_size(axis)
    me = lax.axis_index(axis)
    rows = value.shape[0]
    total = lax.dynamic_slice(value, (0, me * width), (rows, width)).astype(jnp.float32)
    for d in (2, 1, 3):
        piece = lax.dynamic_slice(value, (0, lax.rem(me + d, n) * width), (rows, width))
        total = total + lax.ppermute(piece, axis, shift(n, d)).astype(jnp.float32)
    return total


def reduce_replicas(corrected):
    core = lax.axis_index("c")
    half = corrected.shape[0] // 2
    cols = corrected.shape[1]
    own = lax.dynamic_slice(corrected, (core * half, 0), (half, cols))
    away = lax.dynamic_slice(corrected, ((1 - core) * half, 0), (half, cols))
    got = lax.ppermute(away, "c", SWAP)
    pair = (own.astype(jnp.float32) + got.astype(jnp.float32)).astype(jnp.bfloat16)
    quarter = exchange_sum(pair, "y", cols // 4).astype(jnp.bfloat16)
    return exchange_sum(quarter, "zl", cols // 16).astype(jnp.bfloat16)


def join_cores(value):
    core = lax.axis_index("c")
    got = lax.ppermute(value, "c", SWAP)
    first = jnp.where(core == 0, value, got)
    second = jnp.where(core == 0, got, value)
    return first, second


def sum_chips(value):
    parts = lax.all_to_all(value, CHIPS, 0, 0, tiled=True)
    total = jnp.sum(parts, axis=0, keepdims=True)
    return lax.all_to_all(jnp.broadcast_to(total, value.shape), CHIPS, 0, 0, tiled=True)


def shards(grad, error, q_init):
    replicas = 32
    y, zl = lax.axis_index("y"), lax.axis_index("zl")
    corrected = (grad[0].astype(jnp.float32) + error[0].astype(jnp.float32)).astype(jnp.bfloat16)
    rank = q_init.shape[1]
    mine = reduce_replicas(corrected)
    width = mine.shape[1]
    mean = jnp.concatenate(join_cores(mine), axis=0)
    qt = lax.dynamic_slice(q_init, ((y * 4 + zl) * width, 0), (width, rank)).T
    for step in range(ITERS):
        part = lax.dot_general(qt, mine, (((1,), (1,)), ((), ())), preferred_element_type=jnp.float32)
        part = part.reshape(rank, 4, 128).transpose(1, 0, 2).reshape(4 * rank, 128)
        first, second = join_cores(sum_chips(part))
        left = jnp.concatenate([first, second], axis=0).reshape(8, rank, 128).transpose(1, 0, 2)
        left = left.reshape(rank, ROWS) / replicas
        gram = lax.dot_general(left, left, (((1,), (1,)), ((), ())), precision=lax.Precision.HIGHEST)
        basis = lax.linalg.triangular_solve(jnp.linalg.cholesky(gram), left, left_side=True, lower=True)
        pbt = basis.astype(jnp.bfloat16)
        right = jnp.dot(pbt, mean, preferred_element_type=jnp.float32) / replicas
        qt = right.astype(jnp.bfloat16)
    gathered = lax.all_to_all(
        jnp.broadcast_to(right[None], (16,) + right.shape), ("y", "zl"), 0, 0, tiled=True
    )
    right = gathered.transpose(0, 2, 1).reshape(q_init.shape)
    qb = right.astype(jnp.bfloat16)
    approx = lax.dot_general(pbt, qb, (((0,), (1,)), ((), ())), preferred_element_type=jnp.float32)
    new_error = (corrected.astype(jnp.float32) - approx).astype(jnp.bfloat16)[None]
    own_rows = ROWS // 256
    start = lax.axis_index(("zl", "y", "c", "x", "zh")) * own_rows
    own = lax.dynamic_slice(basis, (0, start), (rank, own_rows)).T
    return (own * math.sqrt(ROWS), right / math.sqrt(ROWS), new_error)


def solution(mesh):
    fine = Mesh(mesh.devices.reshape(4, 4, 2, 4, 2), ("zl", "y", "c", "x", "zh"))
    dp, tensor = ("zl", "y", "c"), ("x", "zh")
    placed = (P(dp, None, tensor), P(dp, None, tensor), P(tensor, None))
    return jax.shard_map(
        shards,
        mesh=fine,
        in_specs=placed,
        out_specs=(P(dp + tensor, None), P(tensor, None), P(dp, None, tensor)),
        check_vma=False,
    )
```

```python
import functools
import math

import jax
import jax.numpy as jnp
import numpy as np
from jax import lax
from jax.experimental import pallas as pl
from jax.experimental.pallas import tpu as pltpu
from jax.sharding import Mesh, PartitionSpec as P

ROWS = 1024
RANK = 32
ITERS = 3
REPLICAS = 32
HEAD = 384
SWAP = [(0, 1), (1, 0)]
CHIPS = ("zl", "y", "x", "zh")
HOLDERS = 128
TILE = 128
SIDE = ROWS // TILE
UPPER = [(i, j) for i in range(SIDE) for j in range(i, SIDE)]
SHARE = len(UPPER) // 2
SLOTS = SHARE + 1
TABLE = np.array([UPPER[:SHARE], UPPER[SHARE:]], np.int32)
VMEM = 40 * 1024 * 1024


def shift(n, d):
    return [(i, (i + d) % n) for i in range(n)]


def exchange_sum(axis, piece):
    n = lax.axis_size(axis)
    me = lax.axis_index(axis)
    total = piece(me).astype(jnp.float32)
    for d in (2, 1, 3):
        sent = piece(lax.rem(me + d, n)).astype(jnp.bfloat16)
        total = total + lax.ppermute(sent, axis, shift(n, d)).astype(jnp.float32)
    return total


def columns(value, start, width):
    return lax.dynamic_slice(value, (0, start), (value.shape[0], width))


def reduce_replicas(grad, error):
    core = lax.axis_index("c")
    total_rows, cols = grad.shape
    half = total_rows // 2
    wide, narrow = cols // 4, cols // 16

    def corrected(start, rows):
        parts = (lax.dynamic_slice(a, (start, 0), (rows, cols)).astype(jnp.float32) for a in (grad, error))
        return sum(parts).astype(jnp.bfloat16)

    def pair(offset, rows):
        got = lax.ppermute(corrected((1 - core) * half + offset, rows), "c", SWAP)
        own = corrected(core * half + offset, rows)
        return own.astype(jnp.float32) + got.astype(jnp.float32)

    tail = pair(HEAD, half - HEAD)
    head = pair(0, HEAD)
    tail = exchange_sum(
        "zl",
        lambda i: jnp.concatenate([columns(tail, j * wide + i * narrow, narrow) for j in range(4)], axis=1),
    )
    head = exchange_sum("y", lambda i: columns(head, i * wide, wide))
    tail = exchange_sum("y", lambda i: columns(tail, i * narrow, narrow))
    head = exchange_sum("zl", lambda i: columns(head, i * narrow, narrow))
    return jnp.concatenate([head, tail], axis=0).astype(jnp.bfloat16)


def join_cores(value):
    core = lax.axis_index("c")
    got = lax.ppermute(value, "c", SWAP)
    return jnp.where(core == 0, value, got), jnp.where(core == 0, got, value)


def dot(a, b, contract, precision=None):
    return lax.dot_general(
        a, b, (contract, ((), ())), precision=precision, preferred_element_type=jnp.float32
    )


def pack_kernel(table, core, total_ref, qt_ref, out_ref):
    def rows(index):
        return total_ref[pl.ds(pl.multiple_of(index * TILE, TILE), TILE), :]

    for k in range(SHARE):
        block = dot(rows(table[k, 0]), rows(table[k, 1]), ((1,), (1,)))
        out_ref[pl.ds(k, TILE, stride=SLOTS), :] = block
    half = ROWS // 2
    for b in range(half // TILE):
        part = dot(qt_ref[...], rows(core[0] * (half // TILE) + b), ((1,), (1,)))
        out_ref[pl.ds(b * RANK * SLOTS + SHARE, RANK, stride=SLOTS), :] = part


def pack(table, core, total, qt):
    return pl.pallas_call(
        pack_kernel,
        out_shape=jax.ShapeDtypeStruct((HOLDERS * SLOTS, TILE), jnp.float32),
        in_specs=[
            pl.BlockSpec(memory_space=pltpu.SMEM),
            pl.BlockSpec(memory_space=pltpu.SMEM),
            pl.BlockSpec(memory_space=pltpu.VMEM),
            pl.BlockSpec(memory_space=pltpu.VMEM),
        ],
        out_specs=pl.BlockSpec(memory_space=pltpu.VMEM),
        compiler_params=pltpu.CompilerParams(vmem_limit_bytes=VMEM),
    )(table, core, total, qt)


def sum_kernel(parts_ref, out_ref):
    for k in range(SLOTS):
        row = jnp.sum(parts_ref[pl.ds(k, HOLDERS, stride=SLOTS), :], axis=0, keepdims=True)
        out_ref[pl.ds(k, HOLDERS, stride=SLOTS), :] = jnp.broadcast_to(row, (HOLDERS, TILE))


def sum_parts(parts):
    return pl.pallas_call(
        sum_kernel,
        out_shape=jax.ShapeDtypeStruct(parts.shape, jnp.float32),
        in_specs=[pl.BlockSpec(memory_space=pltpu.VMEM)],
        out_specs=pl.BlockSpec(memory_space=pltpu.VMEM),
        compiler_params=pltpu.CompilerParams(vmem_limit_bytes=VMEM),
    )(parts)


def inverse_factor(gram):
    shape = (RANK, 2 * RANK)
    row = lax.broadcasted_iota(jnp.int32, shape, 0)
    lane = lax.broadcasted_iota(jnp.int32, shape, 1)
    eye = jnp.where(lane == row + RANK, 1.0, 0.0).astype(jnp.float32)
    work = jnp.concatenate([gram, eye[:, RANK:]], axis=1)
    for j in range(RANK):
        scale = lax.rsqrt(work[j : j + 1, j : j + 1])
        pivot = work[j : j + 1, :] * scale
        column = work[:, j : j + 1] * scale
        work = jnp.where(row > j, work - column * pivot, jnp.where(row == j, pivot, work))
    return work[:, RANK:]


def iterate_kernel(core, own_table, other_table, own_ref, other_ref, total_ref, basis_ref, right_ref, high, low, left_ref):
    half = ROWS // 2
    high_scale = 1.0 / REPLICAS**2
    for table, blocks, place in ((own_table, own_ref, core[0]), (other_table, other_ref, 1 - core[0])):
        for k in range(SHARE):
            i = pl.ds(pl.multiple_of(table[k, 0] * TILE, TILE), TILE)
            j = pl.ds(pl.multiple_of(table[k, 1] * TILE, TILE), TILE)
            block = blocks[pl.ds(k, TILE, stride=SLOTS), :] * high_scale
            for at, value in (((i, j), block), ((j, i), block.T)):
                top = value.astype(jnp.bfloat16)
                high[at] = top
                low[at] = (value - top.astype(jnp.float32)).astype(jnp.bfloat16)
        for b in range(half // TILE):
            at = pl.ds(pl.multiple_of(place * half + b * TILE, TILE), TILE)
            left_ref[:, at] = blocks[pl.ds(b * RANK * SLOTS + SHARE, RANK, stride=SLOTS), :] / REPLICAS
    for step in range(ITERS):
        left = left_ref[...]
        gram = dot(left, left, ((1,), (1,)), lax.Precision.HIGHEST)
        basis = dot(inverse_factor(gram), left, ((1,), (0,)), lax.Precision.HIGHEST)
        pbt = basis.astype(jnp.bfloat16)
        if step < ITERS - 1:
            left_ref[...] = dot(pbt, high[...], ((1,), (0,))) + dot(pbt, low[...], ((1,), (0,)))
    basis_ref[...] = basis
    right_ref[...] = dot(pbt, total_ref[...], ((1,), (0,))) / REPLICAS


def iterate(core, own_table, other_table, own, other, total):
    smem = pl.BlockSpec(memory_space=pltpu.SMEM)
    vmem = pl.BlockSpec(memory_space=pltpu.VMEM)
    return pl.pallas_call(
        iterate_kernel,
        out_shape=(
            jax.ShapeDtypeStruct((RANK, ROWS), jnp.float32),
            jax.ShapeDtypeStruct((RANK, TILE), jnp.float32),
        ),
        in_specs=[smem] * 3 + [vmem] * 3,
        out_specs=(vmem, vmem),
        scratch_shapes=[
            pltpu.VMEM((ROWS, ROWS), jnp.bfloat16),
            pltpu.VMEM((ROWS, ROWS), jnp.bfloat16),
            pltpu.VMEM((RANK, ROWS), jnp.float32),
        ],
        compiler_params=pltpu.CompilerParams(vmem_limit_bytes=VMEM),
    )(core, own_table, other_table, own, other, total)


def over_chips(value):
    value = value.reshape(HOLDERS, SLOTS, 1, TILE)
    return lax.all_to_all(value, CHIPS, 0, 0, tiled=True).reshape(HOLDERS * SLOTS, TILE)


def shards(grad, error, q_init):
    core, y, zl = (lax.axis_index(a) for a in ("c", "y", "zl"))
    mine = reduce_replicas(grad[0], error[0])
    width = mine.shape[1]
    total = jnp.concatenate(join_cores(mine), axis=0)
    qt = lax.dynamic_slice(q_init, ((y * 4 + zl) * width, 0), (width, RANK)).T
    table = jnp.asarray(TABLE)
    own_table = lax.dynamic_index_in_dim(table, core, 0, False)
    other_table = lax.dynamic_index_in_dim(table, 1 - core, 0, False)
    which = core.reshape(1)
    own = over_chips(sum_parts(over_chips(pack(own_table, which, total, qt))))
    other = lax.ppermute(own, "c", SWAP)
    basis, right = iterate(which, own_table, other_table, own, other, total)
    pbt = basis.astype(jnp.bfloat16)
    gathered = lax.all_to_all(
        jnp.broadcast_to(right[None], (16,) + right.shape), ("y", "zl"), 0, 0, tiled=True
    )
    right = gathered.transpose(0, 2, 1).reshape(q_init.shape)
    qb = right.astype(jnp.bfloat16)
    approx = dot(pbt, qb, ((0,), (1,)))
    corrected = (grad[0].astype(jnp.float32) + error[0].astype(jnp.float32)).astype(jnp.bfloat16)
    new_error = (corrected.astype(jnp.float32) - approx).astype(jnp.bfloat16)[None]
    own_rows = ROWS // 256
    start = lax.axis_index(("zl", "y", "c", "x", "zh")) * own_rows
    own_basis = lax.dynamic_slice(basis, (0, start), (RANK, own_rows)).T
    return (own_basis * math.sqrt(ROWS), right / math.sqrt(ROWS), new_error)


def solution(mesh):
    fine = Mesh(mesh.devices.reshape(4, 4, 2, 4, 2), ("zl", "y", "c", "x", "zh"))
    dp, tensor = ("zl", "y", "c"), ("x", "zh")
    placed = (P(dp, None, tensor), P(dp, None, tensor), P(tensor, None))
    return jax.shard_map(
        shards,
        mesh=fine,
        in_specs=placed,
        out_specs=(P(dp + tensor, None), P(tensor, None), P(dp, None, tensor)),
        check_vma=False,
    )
```

```python
import functools
import math

import jax
import jax.numpy as jnp
import numpy as np
from jax import lax
from jax.experimental import pallas as pl
from jax.experimental.pallas import tpu as pltpu
from jax.sharding import Mesh, PartitionSpec as P

ROWS = 1024
RANK = 32
ITERS = 3
PIVOTS = 8
REPLICAS = 32
HEAD = 256
SWAP = [(0, 1), (1, 0)]
PLANE = ("x", "y")
RING = ("zh", "zl")
HOLDERS = 128
RING_SIZE = 8
PLANE_SIZE = HOLDERS // RING_SIZE
TILE = 128
SIDE = ROWS // TILE
UPPER = [(i, j) for i in range(SIDE) for j in range(i, SIDE)]
SHARE = len(UPPER) // 2
SLOTS = SHARE + 1
TABLE = np.array([UPPER[:SHARE], UPPER[SHARE:]], np.int32)
MIB = 1024 * 1024


def shift(n, d):
    return [(i, (i + d) % n) for i in range(n)]


def exchange_sum(axis, piece):
    n = lax.axis_size(axis)
    me = lax.axis_index(axis)
    total = piece(me).astype(jnp.float32)
    for d in (1, 3, 2):
        sent = piece(lax.rem(me + d, n))
        total = total + lax.ppermute(sent, axis, shift(n, d)).astype(jnp.float32)
    return total.astype(jnp.bfloat16)


def columns(value, start, width):
    return lax.dynamic_slice(value, (0, start), (value.shape[0], width))


def add_kernel(place, grad_ref, error_ref, out_ref):
    value = grad_ref[...].astype(jnp.float32) + error_ref[...].astype(jnp.float32)
    out_ref[...] = value.astype(jnp.bfloat16)


def corrected_rows(place, side, first, arrays, rows):
    cols = arrays[0].shape[1]

    def block(i, p):
        return (p[side] * (ROWS // 2 // TILE) + first // TILE + i, 0)

    return pl.pallas_call(
        add_kernel,
        out_shape=jax.ShapeDtypeStruct((rows, cols), jnp.bfloat16),
        grid_spec=pltpu.PrefetchScalarGridSpec(
            num_scalar_prefetch=1,
            grid=(rows // TILE,),
            in_specs=[pl.BlockSpec((TILE, cols), block)] * 2,
            out_specs=pl.BlockSpec((TILE, cols), lambda i, p: (i, 0)),
        ),
        compiler_params=pltpu.CompilerParams(vmem_limit_bytes=16 * MIB),
        cost_estimate=pl.CostEstimate(flops=2 * rows * cols, bytes_accessed=6 * rows * cols, transcendentals=0),
    )(place, *arrays)


def pair_kernel(first, place, own_ref, got_ref, *out_refs):
    rows, width = out_refs[0].shape
    for d, out_ref in enumerate(out_refs):
        at = pl.ds(pl.multiple_of(lax.rem(place[2] + d, 4) * width, width), width)
        own = own_ref[first : first + rows, at].astype(jnp.float32)
        out_ref[...] = (own + got_ref[:, at].astype(jnp.float32)).astype(jnp.bfloat16)


def pair_pieces(place, own, got, first):
    rows, cols = got.shape
    vmem = pl.BlockSpec(memory_space=pltpu.VMEM)
    return pl.pallas_call(
        functools.partial(pair_kernel, first),
        out_shape=[jax.ShapeDtypeStruct((rows, cols // 4), jnp.bfloat16)] * 4,
        in_specs=[pl.BlockSpec(memory_space=pltpu.SMEM), vmem, vmem],
        out_specs=[vmem] * 4,
        compiler_params=pltpu.CompilerParams(vmem_limit_bytes=8 * MIB),
        cost_estimate=pl.CostEstimate(flops=rows * cols, bytes_accessed=6 * rows * cols, transcendentals=0),
    )(place, own, got)


def reduce_replicas(grad, error):
    core, y = lax.axis_index("c"), lax.axis_index("y")
    half, narrow = grad.shape[0] // 2, grad.shape[1] // 16
    place = jnp.stack([1 - core, core, y]).astype(jnp.int32)
    both = (grad, error)

    def rows(side, first, count=HEAD):
        return corrected_rows(place, side, first, both, count)

    got = [lax.ppermute(rows(0, first), "c", SWAP) for first in (0, HEAD)]
    own = rows(1, 0, half)
    pieces = [pair_pieces(place, own, value, k * HEAD) for k, value in enumerate(got)]
    sums = []
    for mine, *others in pieces:
        total = mine.astype(jnp.float32)
        for d in (1, 3, 2):
            total = total + lax.ppermute(others[d - 1], "y", shift(4, d)).astype(jnp.float32)
        sums.append(total.astype(jnp.bfloat16))
    sums = [exchange_sum("zl", lambda i, v=v: columns(v, i * narrow, narrow)) for v in sums]
    return jnp.concatenate(sums, axis=0)


def join_cores(value):
    core = lax.axis_index("c")
    got = lax.ppermute(value, "c", SWAP)
    return jnp.where(core == 0, value, got), jnp.where(core == 0, got, value)


def dot(a, b, contract, precision=None):
    return lax.dot_general(
        a, b, (contract, ((), ())), precision=precision, preferred_element_type=jnp.float32
    )


def pack_kernel(table, core, total_ref, qt_ref, out_ref):
    def rows(index):
        return total_ref[pl.ds(pl.multiple_of(index * TILE, TILE), TILE), :]

    for k in range(SHARE):
        block = dot(rows(table[k, 0]), rows(table[k, 1]), ((1,), (1,)))
        out_ref[pl.ds(k, TILE, stride=SLOTS), :] = block
    half = ROWS // 2
    for b in range(half // TILE):
        part = dot(qt_ref[...], rows(core[0] * (half // TILE) + b), ((1,), (1,)))
        out_ref[pl.ds(b * RANK * SLOTS + SHARE, RANK, stride=SLOTS), :] = part


def pack(table, core, total, qt):
    return pl.pallas_call(
        pack_kernel,
        out_shape=jax.ShapeDtypeStruct((HOLDERS * SLOTS, TILE), jnp.float32),
        in_specs=[
            pl.BlockSpec(memory_space=pltpu.SMEM),
            pl.BlockSpec(memory_space=pltpu.SMEM),
            pl.BlockSpec(memory_space=pltpu.VMEM),
            pl.BlockSpec(memory_space=pltpu.VMEM),
        ],
        out_specs=pl.BlockSpec(memory_space=pltpu.VMEM),
        compiler_params=pltpu.CompilerParams(vmem_limit_bytes=4 * MIB),
    )(table, core, total, qt)


def small_kernel(body, rows, *args):
    vmem = pl.BlockSpec(memory_space=pltpu.VMEM)
    return pl.pallas_call(
        body,
        out_shape=jax.ShapeDtypeStruct((rows, TILE), jnp.float32),
        in_specs=[vmem],
        out_specs=vmem,
        compiler_params=pltpu.CompilerParams(vmem_limit_bytes=4 * MIB),
    )(*args)


def sum_kernel(parts_ref, out_ref):
    rows = RING_SIZE * SLOTS
    total = parts_ref[:rows, :]
    for p in range(1, parts_ref.shape[0] // rows):
        total = total + parts_ref[p * rows : (p + 1) * rows, :]
    for p in range(out_ref.shape[0] // rows):
        out_ref[p * rows : (p + 1) * rows, :] = total


def ring_kernel(parts_ref, out_ref):
    for k in range(SLOTS):
        row = jnp.sum(parts_ref[pl.ds(k, RING_SIZE, stride=SLOTS), :], axis=0, keepdims=True)
        out_ref[pl.ds(k, RING_SIZE, stride=SLOTS), :] = jnp.broadcast_to(row, (RING_SIZE, TILE))


def inverse_factor(gram):
    wide = (RANK, 2 * RANK)
    row = lax.broadcasted_iota(jnp.int32, wide, 0)
    lane = lax.broadcasted_iota(jnp.int32, wide, 1)
    eye = jnp.where(lane == row + RANK, 1.0, 0.0).astype(jnp.float32)
    work = jnp.concatenate([gram, eye[:, RANK:]], axis=1)
    result = jnp.zeros(wide, jnp.float32)
    for j in range(0, RANK, PIVOTS):
        rows = [work[j + a : j + a + 1, :] for a in range(PIVOTS)]
        cols = [jnp.broadcast_to(work[:, j + a : j + a + 1], wide) for a in range(PIVOTS)]
        corner = {
            (a, b): jnp.broadcast_to(work[j + a : j + a + 1, j + b : j + b + 1], (1, 2 * RANK))
            for a in range(PIVOTS)
            for b in range(a, PIVOTS)
        }
        for a in range(PIVOTS):
            inverse = 1.0 / corner[a, a]
            result = jnp.where(row == j + a, rows[a] * lax.rsqrt(corner[a, a]), result)
            for b in range(a + 1, PIVOTS):
                factor = corner[a, b] * inverse
                rows[b] = rows[b] - factor * rows[a]
                cols[b] = cols[b] - cols[a] * factor
                for c in range(b, PIVOTS):
                    corner[b, c] = corner[b, c] - factor * corner[a, c]
            cols[a] = cols[a] * inverse
        if j + PIVOTS < RANK:
            work = work - sum(cols[a] * rows[a] for a in range(PIVOTS))
    return result[:, RANK:]


def normal_kernel(left):
    gram = dot(left, left, ((1,), (1,)), lax.Precision.HIGHEST)
    inverse = inverse_factor(gram)
    return inverse, dot(inverse, left, ((1,), (0,)), lax.Precision.HIGHEST)


def iterate_kernel(core, own_table, other_table, own_ref, other_ref, total_ref, last_ref, spread_ref, high, low, left_ref):
    half = ROWS // 2
    high_scale = 1.0 / REPLICAS**2
    for table, blocks, place in ((own_table, own_ref, core[0]), (other_table, other_ref, 1 - core[0])):
        for k in range(SHARE):
            i = pl.ds(pl.multiple_of(table[k, 0] * TILE, TILE), TILE)
            j = pl.ds(pl.multiple_of(table[k, 1] * TILE, TILE), TILE)
            block = blocks[pl.ds(k, TILE, stride=SLOTS), :] * high_scale
            for at, value in (((i, j), block), ((j, i), block.T)):
                top = value.astype(jnp.bfloat16)
                high[at] = top
                low[at] = (value - top.astype(jnp.float32)).astype(jnp.bfloat16)
        for b in range(half // TILE):
            at = pl.ds(pl.multiple_of(place * half + b * TILE, TILE), TILE)
            left_ref[:, at] = blocks[pl.ds(b * RANK * SLOTS + SHARE, RANK, stride=SLOTS), :] / REPLICAS
    left = left_ref[...]
    for step in range(ITERS - 1):
        basis = normal_kernel(left)[1]
        pbt = basis.astype(jnp.bfloat16)
        left = dot(pbt, high[...], ((1,), (0,))) + dot(pbt, low[...], ((1,), (0,)))
    last_ref[...] = left
    total = total_ref[...].astype(jnp.float32)
    spread = dot(left, total, ((1,), (0,)), lax.Precision.HIGHEST) / REPLICAS
    for p in range(spread_ref.shape[0]):
        spread_ref[p] = spread


def iterate(core, own_table, other_table, own, other, total):
    smem = pl.BlockSpec(memory_space=pltpu.SMEM)
    vmem = pl.BlockSpec(memory_space=pltpu.VMEM)
    return pl.pallas_call(
        iterate_kernel,
        out_shape=(
            jax.ShapeDtypeStruct((RANK, ROWS), jnp.float32),
            jax.ShapeDtypeStruct((16, RANK, TILE), jnp.float32),
        ),
        in_specs=[smem] * 3 + [vmem] * 3,
        out_specs=(vmem, vmem),
        scratch_shapes=[
            pltpu.VMEM((ROWS, ROWS), jnp.bfloat16),
            pltpu.VMEM((ROWS, ROWS), jnp.bfloat16),
            pltpu.VMEM((RANK, ROWS), jnp.float32),
        ],
        compiler_params=pltpu.CompilerParams(vmem_limit_bytes=14 * MIB),
    )(core, own_table, other_table, own, other, total)


def last_kernel(left_ref, inverse_ref, basis_ref):
    inverse_ref[...], basis_ref[...] = normal_kernel(left_ref[...])


def last_basis(left):
    vmem = pl.BlockSpec(memory_space=pltpu.VMEM)
    return pl.pallas_call(
        last_kernel,
        out_shape=(
            jax.ShapeDtypeStruct((RANK, RANK), jnp.float32),
            jax.ShapeDtypeStruct(left.shape, jnp.float32),
        ),
        in_specs=[vmem],
        out_specs=(vmem, vmem),
        compiler_params=pltpu.CompilerParams(vmem_limit_bytes=4 * MIB),
        cost_estimate=pl.CostEstimate(flops=1000, bytes_accessed=1000, transcendentals=0),
    )(left)


def corrected_kernel(grad_ref, error_ref, out_ref):
    value = grad_ref[...].astype(jnp.float32) + error_ref[...].astype(jnp.float32)
    out_ref[...] = value.astype(jnp.bfloat16)


def corrected_sum(grad, error):
    rows = pl.BlockSpec((2 * TILE, grad.shape[1]), lambda i: (i, 0))
    return pl.pallas_call(
        corrected_kernel,
        out_shape=jax.ShapeDtypeStruct(grad.shape, grad.dtype),
        grid=(ROWS // TILE // 2,),
        in_specs=[rows, rows],
        out_specs=rows,
        compiler_params=pltpu.CompilerParams(vmem_limit_bytes=60 * MIB),
        cost_estimate=pl.CostEstimate(flops=1000, bytes_accessed=1000, transcendentals=0),
    )(grad, error)


def finish_kernel(inverse_ref, spread_ref, pbt_ref, corrected_ref, factor_ref, out_ref, wide, qbt):
    blocks, _, width = spread_ref.shape
    step = pl.program_id(0)

    @pl.when(step == 0)
    def _():
        for b in range(blocks):
            wide[:, b * width : (b + 1) * width] = spread_ref[b]
        right = dot(inverse_ref[...], wide[...], ((1,), (0,)), lax.Precision.HIGHEST)
        factor_ref[...] = right / math.sqrt(ROWS)
        qbt[...] = right.astype(jnp.bfloat16)

    rows = out_ref.shape[0]
    approx = dot(pbt_ref[...], qbt[...], ((0,), (0,)))
    corrected = corrected_ref[pl.ds(pl.multiple_of(step * rows, rows), rows), :]
    out_ref[...] = (corrected.astype(jnp.float32) - approx).astype(jnp.bfloat16)


def finish(inverse, spread, pbt, corrected):
    vmem = pl.BlockSpec(memory_space=pltpu.VMEM)
    cols = corrected.shape[1]
    rows = 2 * TILE
    return pl.pallas_call(
        finish_kernel,
        out_shape=(
            jax.ShapeDtypeStruct((RANK, cols), jnp.float32),
            jax.ShapeDtypeStruct((ROWS, cols), jnp.bfloat16),
        ),
        grid=(ROWS // rows,),
        in_specs=[vmem, vmem, pl.BlockSpec((RANK, rows), lambda i: (0, i)), vmem],
        out_specs=(pl.BlockSpec((RANK, cols), lambda i: (0, 0)), pl.BlockSpec((rows, cols), lambda i: (i, 0))),
        scratch_shapes=[pltpu.VMEM((RANK, cols), jnp.float32), pltpu.VMEM((RANK, cols), jnp.bfloat16)],
        compiler_params=pltpu.CompilerParams(vmem_limit_bytes=16 * MIB),
    )(inverse, spread, pbt, corrected)


def sum_chips(value):
    rows = RING_SIZE * SLOTS

    def swap(v, axes, size):
        v = lax.all_to_all(v.reshape(size, rows, TILE), axes, 0, 0, tiled=True)
        return v.reshape(size * rows, TILE)

    def ring(v):
        v = lax.all_to_all(v.reshape(RING_SIZE, SLOTS, 1, TILE), RING, 0, 0, tiled=True)
        return v.reshape(rows, TILE)

    part = small_kernel(sum_kernel, rows, swap(value, PLANE, PLANE_SIZE))
    part = ring(small_kernel(ring_kernel, rows, ring(part)))
    return swap(small_kernel(sum_kernel, PLANE_SIZE * rows, part), PLANE, PLANE_SIZE)


def shards(grad, error, q_init):
    core, y, zl = (lax.axis_index(a) for a in ("c", "y", "zl"))
    mine = reduce_replicas(grad[0], error[0])
    width = mine.shape[1]
    total = jnp.concatenate(join_cores(mine), axis=0)
    qt = lax.dynamic_slice(q_init, ((y * 4 + zl) * width, 0), (width, RANK)).T
    table = jnp.asarray(TABLE)
    own_table = lax.dynamic_index_in_dim(table, core, 0, False)
    other_table = lax.dynamic_index_in_dim(table, 1 - core, 0, False)
    which = core.reshape(1)
    packed = pack(own_table, which, total, qt)
    grad, error, packed = lax.optimization_barrier((grad, error, packed))
    corrected = corrected_sum(grad[0], error[0])
    own, corrected = lax.optimization_barrier((sum_chips(packed), corrected))
    other = lax.ppermute(own, "c", SWAP)
    left, spread = iterate(which, own_table, other_table, own, other, total)
    spread = lax.all_to_all(spread, ("y", "zl"), 0, 0, tiled=True)
    inverse, basis = last_basis(left)
    factor, new_error = finish(inverse, spread, basis.astype(jnp.bfloat16), corrected)
    own_rows = ROWS // 256
    start = lax.axis_index(("zl", "y", "c", "x", "zh")) * own_rows
    own_basis = lax.dynamic_slice(basis, (0, start), (RANK, own_rows)).T
    return (own_basis * math.sqrt(ROWS), factor.T, new_error[None])


def solution(mesh):
    fine = Mesh(mesh.devices.reshape(4, 4, 2, 4, 2), ("zl", "y", "c", "x", "zh"))
    dp, tensor = ("zl", "y", "c"), ("x", "zh")
    placed = (P(dp, None, tensor), P(dp, None, tensor), P(tensor, None))
    return jax.shard_map(
        shards,
        mesh=fine,
        in_specs=placed,
        out_specs=(P(dp + tensor, None), P(tensor, None), P(dp, None, tensor)),
        check_vma=False,
    )
```

```python
import functools
import math

import jax
import jax.numpy as jnp
import numpy as np
from jax import lax
from jax.experimental import pallas as pl
from jax.experimental.pallas import tpu as pltpu
from jax.sharding import Mesh, PartitionSpec as P

ROWS = 1024
RANK = 32
ITERS = 3
PIVOTS = 8
REPLICAS = 32
HEAD = 256
SWAP = [(0, 1), (1, 0)]
PLANE = ("x", "y")
RING = ("zh", "zl")
HOLDERS = 128
RING_SIZE = 8
PLANE_SIZE = HOLDERS // RING_SIZE
TILE = 128
SIDE = ROWS // TILE
UPPER = [(i, j) for i in range(SIDE) for j in range(i, SIDE)]
SHARE = len(UPPER) // 2
SLOTS = SHARE + 1
TABLE = np.array([UPPER[:SHARE], UPPER[SHARE:]], np.int32)
MIB = 1024 * 1024


def shift(n, d):
    return [(i, (i + d) % n) for i in range(n)]


def exchange_sum(axis, piece):
    n = lax.axis_size(axis)
    me = lax.axis_index(axis)
    total = piece(me).astype(jnp.float32)
    for d in (1, 3, 2):
        sent = piece(lax.rem(me + d, n))
        total = total + lax.ppermute(sent, axis, shift(n, d)).astype(jnp.float32)
    return total.astype(jnp.bfloat16)


def columns(value, start, width):
    return lax.dynamic_slice(value, (0, start), (value.shape[0], width))


def add_kernel(place, grad_ref, error_ref, out_ref):
    value = grad_ref[...].astype(jnp.float32) + error_ref[...].astype(jnp.float32)
    out_ref[...] = value.astype(jnp.bfloat16)


def corrected_rows(place, side, first, arrays, rows):
    cols = arrays[0].shape[1]

    def block(i, p):
        return (p[side] * (ROWS // 2 // TILE) + first // TILE + i, 0)

    return pl.pallas_call(
        add_kernel,
        out_shape=jax.ShapeDtypeStruct((rows, cols), jnp.bfloat16),
        grid_spec=pltpu.PrefetchScalarGridSpec(
            num_scalar_prefetch=1,
            grid=(rows // TILE,),
            in_specs=[pl.BlockSpec((TILE, cols), block)] * 2,
            out_specs=pl.BlockSpec((TILE, cols), lambda i, p: (i, 0)),
        ),
        compiler_params=pltpu.CompilerParams(vmem_limit_bytes=16 * MIB),
        cost_estimate=pl.CostEstimate(flops=2 * rows * cols, bytes_accessed=6 * rows * cols, transcendentals=0),
    )(place, *arrays)


def pair_kernel(first, place, own_ref, got_ref, *out_refs):
    rows, width = out_refs[0].shape
    for d, out_ref in enumerate(out_refs):
        at = pl.ds(pl.multiple_of(lax.rem(place[2] + d, 4) * width, width), width)
        own = own_ref[first : first + rows, at].astype(jnp.float32)
        out_ref[...] = (own + got_ref[:, at].astype(jnp.float32)).astype(jnp.bfloat16)


def pair_pieces(place, own, got, first):
    rows, cols = got.shape
    vmem = pl.BlockSpec(memory_space=pltpu.VMEM)
    return pl.pallas_call(
        functools.partial(pair_kernel, first),
        out_shape=[jax.ShapeDtypeStruct((rows, cols // 4), jnp.bfloat16)] * 4,
        in_specs=[pl.BlockSpec(memory_space=pltpu.SMEM), vmem, vmem],
        out_specs=[vmem] * 4,
        compiler_params=pltpu.CompilerParams(vmem_limit_bytes=8 * MIB),
        cost_estimate=pl.CostEstimate(flops=rows * cols, bytes_accessed=6 * rows * cols, transcendentals=0),
    )(place, own, got)


def reduce_replicas(grad, error):
    core, y = lax.axis_index("c"), lax.axis_index("y")
    half, narrow = grad.shape[0] // 2, grad.shape[1] // 16
    place = jnp.stack([1 - core, core, y]).astype(jnp.int32)
    both = (grad, error)

    def rows(side, first, count=HEAD):
        return corrected_rows(place, side, first, both, count)

    got = [lax.ppermute(rows(0, first), "c", SWAP) for first in (0, HEAD)]
    own = rows(1, 0, half)
    pieces = [pair_pieces(place, own, value, k * HEAD) for k, value in enumerate(got)]
    sums = []
    for mine, *others in pieces:
        total = mine.astype(jnp.float32)
        for d in (1, 3, 2):
            total = total + lax.ppermute(others[d - 1], "y", shift(4, d)).astype(jnp.float32)
        sums.append(total.astype(jnp.bfloat16))
    sums = [exchange_sum("zl", lambda i, v=v: columns(v, i * narrow, narrow)) for v in sums]
    return jnp.concatenate(sums, axis=0)


def join_cores(value):
    core = lax.axis_index("c")
    got = lax.ppermute(value, "c", SWAP)
    return jnp.where(core == 0, value, got), jnp.where(core == 0, got, value)


def dot(a, b, contract, precision=None):
    return lax.dot_general(
        a, b, (contract, ((), ())), precision=precision, preferred_element_type=jnp.float32
    )


def pack_kernel(table, core, total_ref, qt_ref, out_ref):
    def rows(index):
        return total_ref[pl.ds(pl.multiple_of(index * TILE, TILE), TILE), :]

    for k in range(SHARE):
        block = dot(rows(table[k, 0]), rows(table[k, 1]), ((1,), (1,)))
        out_ref[pl.ds(k, TILE, stride=SLOTS), :] = block
    half = ROWS // 2
    for b in range(half // TILE):
        part = dot(qt_ref[...], rows(core[0] * (half // TILE) + b), ((1,), (1,)))
        out_ref[pl.ds(b * RANK * SLOTS + SHARE, RANK, stride=SLOTS), :] = part


def pack(table, core, total, qt):
    return pl.pallas_call(
        pack_kernel,
        out_shape=jax.ShapeDtypeStruct((HOLDERS * SLOTS, TILE), jnp.float32),
        in_specs=[
            pl.BlockSpec(memory_space=pltpu.SMEM),
            pl.BlockSpec(memory_space=pltpu.SMEM),
            pl.BlockSpec(memory_space=pltpu.VMEM),
            pl.BlockSpec(memory_space=pltpu.VMEM),
        ],
        out_specs=pl.BlockSpec(memory_space=pltpu.VMEM),
        compiler_params=pltpu.CompilerParams(vmem_limit_bytes=4 * MIB),
    )(table, core, total, qt)


def small_kernel(body, rows, *args):
    vmem = pl.BlockSpec(memory_space=pltpu.VMEM)
    return pl.pallas_call(
        body,
        out_shape=jax.ShapeDtypeStruct((rows, TILE), jnp.float32),
        in_specs=[vmem],
        out_specs=vmem,
        compiler_params=pltpu.CompilerParams(vmem_limit_bytes=4 * MIB),
    )(*args)


def sum_kernel(parts_ref, out_ref):
    rows = RING_SIZE * SLOTS
    total = parts_ref[:rows, :]
    for p in range(1, parts_ref.shape[0] // rows):
        total = total + parts_ref[p * rows : (p + 1) * rows, :]
    for p in range(out_ref.shape[0] // rows):
        out_ref[p * rows : (p + 1) * rows, :] = total


def ring_kernel(parts_ref, out_ref):
    for k in range(SLOTS):
        row = jnp.sum(parts_ref[pl.ds(k, RING_SIZE, stride=SLOTS), :], axis=0, keepdims=True)
        out_ref[pl.ds(k, RING_SIZE, stride=SLOTS), :] = jnp.broadcast_to(row, (RING_SIZE, TILE))


def inverse_factor(gram):
    wide = (RANK, 2 * RANK)
    row = lax.broadcasted_iota(jnp.int32, wide, 0)
    lane = lax.broadcasted_iota(jnp.int32, wide, 1)
    eye = jnp.where(lane == row + RANK, 1.0, 0.0).astype(jnp.float32)
    work = jnp.concatenate([gram, eye[:, RANK:]], axis=1)
    result = jnp.zeros(wide, jnp.float32)
    for j in range(0, RANK, PIVOTS):
        rows = [work[j + a : j + a + 1, :] for a in range(PIVOTS)]
        cols = [jnp.broadcast_to(work[:, j + a : j + a + 1], wide) for a in range(PIVOTS)]
        corner = {
            (a, b): jnp.broadcast_to(work[j + a : j + a + 1, j + b : j + b + 1], (1, 2 * RANK))
            for a in range(PIVOTS)
            for b in range(a, PIVOTS)
        }
        for a in range(PIVOTS):
            inverse = 1.0 / corner[a, a]
            result = jnp.where(row == j + a, rows[a] * lax.rsqrt(corner[a, a]), result)
            for b in range(a + 1, PIVOTS):
                factor = corner[a, b] * inverse
                rows[b] = rows[b] - factor * rows[a]
                cols[b] = cols[b] - cols[a] * factor
                for c in range(b, PIVOTS):
                    corner[b, c] = corner[b, c] - factor * corner[a, c]
            cols[a] = cols[a] * inverse
        if j + PIVOTS < RANK:
            work = work - sum(cols[a] * rows[a] for a in range(PIVOTS))
    return result[:, RANK:]


def normal_kernel(left):
    gram = dot(left, left, ((1,), (1,)), lax.Precision.HIGHEST)
    inverse = inverse_factor(gram)
    return inverse, dot(inverse, left, ((1,), (0,)), lax.Precision.HIGHEST)


def iterate_kernel(core, own_table, other_table, own_ref, other_ref, total_ref, near_ref, across_ref, last_ref, spread_ref, high, low, left_ref):
    half = ROWS // 2
    high_scale = 1.0 / REPLICAS**2
    for table, blocks, place in ((own_table, own_ref, core[0]), (other_table, other_ref, 1 - core[0])):
        for k in range(SHARE):
            i = pl.ds(pl.multiple_of(table[k, 0] * TILE, TILE), TILE)
            j = pl.ds(pl.multiple_of(table[k, 1] * TILE, TILE), TILE)
            block = blocks[pl.ds(k, TILE, stride=SLOTS), :] * high_scale
            for at, value in (((i, j), block), ((j, i), block.T)):
                top = value.astype(jnp.bfloat16)
                high[at] = top
                low[at] = (value - top.astype(jnp.float32)).astype(jnp.bfloat16)
        for b in range(half // TILE):
            at = pl.ds(pl.multiple_of(place * half + b * TILE, TILE), TILE)
            left_ref[:, at] = blocks[pl.ds(b * RANK * SLOTS + SHARE, RANK, stride=SLOTS), :] / REPLICAS
    left = left_ref[...]
    for step in range(ITERS - 1):
        basis = normal_kernel(left)[1]
        pbt = basis.astype(jnp.bfloat16)
        left = dot(pbt, high[...], ((1,), (0,))) + dot(pbt, low[...], ((1,), (0,)))
    last_ref[...] = left
    left_ref[...] = left

    def product(part, columns_ref):
        return dot(part, columns_ref.astype(jnp.float32), ((1,), (0,)), lax.Precision.HIGHEST)

    spread_ref[0] = product(left, total_ref[...]) / REPLICAS
    halves = [left_ref[:, pl.ds(pl.multiple_of(side * half, half), half)] for side in (core[0], 1 - core[0])]
    for k in range(near_ref.shape[0]):
        spread_ref[k + 1] = (product(halves[0], near_ref[k]) + product(halves[1], across_ref[k])) / REPLICAS


def iterate(core, own_table, other_table, own, other, total, near, across):
    smem = pl.BlockSpec(memory_space=pltpu.SMEM)
    vmem = pl.BlockSpec(memory_space=pltpu.VMEM)
    return pl.pallas_call(
        iterate_kernel,
        out_shape=(
            jax.ShapeDtypeStruct((RANK, ROWS), jnp.float32),
            jax.ShapeDtypeStruct((4, RANK, TILE), jnp.float32),
        ),
        in_specs=[smem] * 3 + [vmem] * 5,
        out_specs=(vmem, vmem),
        scratch_shapes=[
            pltpu.VMEM((ROWS, ROWS), jnp.bfloat16),
            pltpu.VMEM((ROWS, ROWS), jnp.bfloat16),
            pltpu.VMEM((RANK, ROWS), jnp.float32),
        ],
        compiler_params=pltpu.CompilerParams(vmem_limit_bytes=14 * MIB),
    )(core, own_table, other_table, own, other, total, near, across)


def last_kernel(left_ref, inverse_ref, basis_ref):
    inverse_ref[...], basis_ref[...] = normal_kernel(left_ref[...])


def last_basis(left):
    vmem = pl.BlockSpec(memory_space=pltpu.VMEM)
    return pl.pallas_call(
        last_kernel,
        out_shape=(
            jax.ShapeDtypeStruct((RANK, RANK), jnp.float32),
            jax.ShapeDtypeStruct(left.shape, jnp.float32),
        ),
        in_specs=[vmem],
        out_specs=(vmem, vmem),
        compiler_params=pltpu.CompilerParams(vmem_limit_bytes=4 * MIB),
        cost_estimate=pl.CostEstimate(flops=1000, bytes_accessed=1000, transcendentals=0),
    )(left)


def corrected_kernel(grad_ref, error_ref, out_ref):
    value = grad_ref[...].astype(jnp.float32) + error_ref[...].astype(jnp.float32)
    out_ref[...] = value.astype(jnp.bfloat16)


def corrected_sum(grad, error):
    rows = pl.BlockSpec((2 * TILE, grad.shape[1]), lambda i: (i, 0))
    return pl.pallas_call(
        corrected_kernel,
        out_shape=jax.ShapeDtypeStruct(grad.shape, grad.dtype),
        grid=(ROWS // TILE // 2,),
        in_specs=[rows, rows],
        out_specs=rows,
        compiler_params=pltpu.CompilerParams(vmem_limit_bytes=60 * MIB),
        cost_estimate=pl.CostEstimate(flops=1000, bytes_accessed=1000, transcendentals=0),
    )(grad, error)


def finish_kernel(place, inverse_ref, *refs):
    *spread_refs, pbt_ref, corrected_ref, factor_ref, out_ref, wide, qbt = refs
    step = pl.program_id(0)

    @pl.when(step == 0)
    def _():
        for d, spread_ref in enumerate(spread_refs):
            blocks, _, width = spread_ref.shape
            for k in range(blocks):
                block = lax.rem(place[0] + 4 - d, 4) * blocks + lax.rem(place[1] + blocks - k, blocks)
                wide[:, pl.ds(pl.multiple_of(block * width, width), width)] = spread_ref[k]
        right = dot(inverse_ref[...], wide[...], ((1,), (0,)), lax.Precision.HIGHEST)
        factor_ref[...] = right / math.sqrt(ROWS)
        qbt[...] = right.astype(jnp.bfloat16)

    rows = out_ref.shape[0]
    approx = dot(pbt_ref[...], qbt[...], ((0,), (0,)))
    corrected = corrected_ref[pl.ds(pl.multiple_of(step * rows, rows), rows), :]
    out_ref[...] = (corrected.astype(jnp.float32) - approx).astype(jnp.bfloat16)


def finish(place, inverse, spreads, pbt, corrected):
    vmem = pl.BlockSpec(memory_space=pltpu.VMEM)
    cols = corrected.shape[1]
    rows = 2 * TILE
    return pl.pallas_call(
        finish_kernel,
        out_shape=(
            jax.ShapeDtypeStruct((RANK, cols), jnp.float32),
            jax.ShapeDtypeStruct((ROWS, cols), jnp.bfloat16),
        ),
        grid=(ROWS // rows,),
        in_specs=[pl.BlockSpec(memory_space=pltpu.SMEM), vmem]
        + [vmem] * len(spreads)
        + [pl.BlockSpec((RANK, rows), lambda i: (0, i)), vmem],
        out_specs=(pl.BlockSpec((RANK, cols), lambda i: (0, 0)), pl.BlockSpec((rows, cols), lambda i: (i, 0))),
        scratch_shapes=[pltpu.VMEM((RANK, cols), jnp.float32), pltpu.VMEM((RANK, cols), jnp.bfloat16)],
        compiler_params=pltpu.CompilerParams(vmem_limit_bytes=16 * MIB),
    )(place, inverse, *spreads, pbt, corrected)


def sum_chips(value, later):
    rows = RING_SIZE * SLOTS

    def swap(v, axes, size):
        v = lax.all_to_all(v.reshape(size, rows, TILE), axes, 0, 0, tiled=True)
        return v.reshape(size * rows, TILE)

    def ring(v):
        v = lax.all_to_all(v.reshape(RING_SIZE, SLOTS, 1, TILE), RING, 0, 0, tiled=True)
        return v.reshape(rows, TILE)

    part = small_kernel(sum_kernel, rows, swap(value, PLANE, PLANE_SIZE))
    part = ring(small_kernel(ring_kernel, rows, ring(part)))
    part, later = lax.optimization_barrier((part, later))
    return swap(small_kernel(sum_kernel, PLANE_SIZE * rows, part), PLANE, PLANE_SIZE), later


def shards(grad, error, q_init):
    core, y, zl = (lax.axis_index(a) for a in ("c", "y", "zl"))
    mine = reduce_replicas(grad[0], error[0])
    width = mine.shape[1]
    total = jnp.concatenate(join_cores(mine), axis=0)
    qt = lax.dynamic_slice(q_init, ((y * 4 + zl) * width, 0), (width, RANK)).T
    table = jnp.asarray(TABLE)
    own_table = lax.dynamic_index_in_dim(table, core, 0, False)
    other_table = lax.dynamic_index_in_dim(table, 1 - core, 0, False)
    which = core.reshape(1)
    packed = pack(own_table, which, total, qt)
    grad, error, packed = lax.optimization_barrier((grad, error, packed))
    corrected = corrected_sum(grad[0], error[0])
    own, mine = sum_chips(packed, mine)
    near = {d: lax.ppermute(mine, "zl", shift(4, d)) for d in (1, 3, 2)}
    near = jnp.stack([near[1], near[2], near[3]])
    own, corrected, near = lax.optimization_barrier((own, corrected, near))
    across = lax.ppermute(near, "c", SWAP)
    other = lax.ppermute(own, "c", SWAP)
    left, spread = iterate(which, own_table, other_table, own, other, total, near, across)
    spreads = {d: lax.ppermute(spread, "y", shift(4, d)) for d in (1, 3, 2)}
    spreads = [spread, spreads[1], spreads[2], spreads[3]]
    inverse, basis = last_basis(left)
    factor, new_error = finish(jnp.stack([y, zl]), inverse, spreads, basis.astype(jnp.bfloat16), corrected)
    own_rows = ROWS // 256
    start = lax.axis_index(("zl", "y", "c", "x", "zh")) * own_rows
    own_basis = lax.dynamic_slice(basis, (0, start), (RANK, own_rows)).T
    return (own_basis * math.sqrt(ROWS), factor.T, new_error[None])


def solution(mesh):
    fine = Mesh(mesh.devices.reshape(4, 4, 2, 4, 2), ("zl", "y", "c", "x", "zh"))
    dp, tensor = ("zl", "y", "c"), ("x", "zh")
    placed = (P(dp, None, tensor), P(dp, None, tensor), P(tensor, None))
    return jax.shard_map(
        shards,
        mesh=fine,
        in_specs=placed,
        out_specs=(P(dp + tensor, None), P(tensor, None), P(dp, None, tensor)),
        check_vma=False,
    )
```

```python
import functools
import math

import jax
import jax.numpy as jnp
import numpy as np
from jax import lax
from jax.experimental import pallas as pl
from jax.experimental.pallas import tpu as pltpu
from jax.sharding import Mesh, PartitionSpec as P

ROWS = 1024
RANK = 32
ITERS = 3
PIVOTS = 8
REPLICAS = 32
HEAD = 256
SWAP = [(0, 1), (1, 0)]
PLANE = ("x", "y")
RING = ("zh", "zl")
HOLDERS = 128
RING_SIZE = 8
PLANE_SIZE = HOLDERS // RING_SIZE
TILE = 128
SIDE = ROWS // TILE
UPPER = [(i, j) for i in range(SIDE) for j in range(i, SIDE)]
SHARE = len(UPPER) // 2
SLOTS = SHARE + 1
TABLE = np.array([UPPER[:SHARE], UPPER[SHARE:]], np.int32)
MIB = 1024 * 1024


def shift(n, d):
    return [(i, (i + d) % n) for i in range(n)]


def exchange_sum(axis, piece):
    n = lax.axis_size(axis)
    me = lax.axis_index(axis)
    total = piece(me).astype(jnp.float32)
    for d in (1, 3, 2):
        sent = piece(lax.rem(me + d, n))
        total = total + lax.ppermute(sent, axis, shift(n, d)).astype(jnp.float32)
    return total.astype(jnp.bfloat16)


def columns(value, start, width):
    return lax.dynamic_slice(value, (0, start), (value.shape[0], width))


def add_kernel(place, grad_ref, error_ref, out_ref):
    value = grad_ref[...].astype(jnp.float32) + error_ref[...].astype(jnp.float32)
    out_ref[...] = value.astype(jnp.bfloat16)


def corrected_rows(place, side, first, arrays, rows):
    cols = arrays[0].shape[1]

    def block(i, p):
        return (p[side] * (ROWS // 2 // TILE) + first // TILE + i, 0)

    return pl.pallas_call(
        add_kernel,
        out_shape=jax.ShapeDtypeStruct((rows, cols), jnp.bfloat16),
        grid_spec=pltpu.PrefetchScalarGridSpec(
            num_scalar_prefetch=1,
            grid=(rows // TILE,),
            in_specs=[pl.BlockSpec((TILE, cols), block)] * 2,
            out_specs=pl.BlockSpec((TILE, cols), lambda i, p: (i, 0)),
        ),
        compiler_params=pltpu.CompilerParams(vmem_limit_bytes=16 * MIB),
        cost_estimate=pl.CostEstimate(flops=2 * rows * cols, bytes_accessed=6 * rows * cols, transcendentals=0),
    )(place, *arrays)


def pair_kernel(first, place, own_ref, got_ref, *out_refs):
    rows, width = out_refs[0].shape
    for d, out_ref in enumerate(out_refs):
        at = pl.ds(pl.multiple_of(lax.rem(place[2] + d, 4) * width, width), width)
        own = own_ref[first : first + rows, at].astype(jnp.float32)
        out_ref[...] = (own + got_ref[:, at].astype(jnp.float32)).astype(jnp.bfloat16)


def pair_pieces(place, own, got, first):
    rows, cols = got.shape
    vmem = pl.BlockSpec(memory_space=pltpu.VMEM)
    return pl.pallas_call(
        functools.partial(pair_kernel, first),
        out_shape=[jax.ShapeDtypeStruct((rows, cols // 4), jnp.bfloat16)] * 4,
        in_specs=[pl.BlockSpec(memory_space=pltpu.SMEM), vmem, vmem],
        out_specs=[vmem] * 4,
        compiler_params=pltpu.CompilerParams(vmem_limit_bytes=8 * MIB),
        cost_estimate=pl.CostEstimate(flops=rows * cols, bytes_accessed=6 * rows * cols, transcendentals=0),
    )(place, own, got)


def reduce_replicas(grad, error):
    core, y = lax.axis_index("c"), lax.axis_index("y")
    half, narrow = grad.shape[0] // 2, grad.shape[1] // 16
    place = jnp.stack([1 - core, core, y]).astype(jnp.int32)
    both = (grad, error)

    def rows(side, first, count=HEAD):
        return corrected_rows(place, side, first, both, count)

    got = [lax.ppermute(rows(0, first), "c", SWAP) for first in (0, HEAD)]
    own = rows(1, 0, half)
    pieces = [pair_pieces(place, own, value, k * HEAD) for k, value in enumerate(got)]
    sums = []
    for mine, *others in pieces:
        total = mine.astype(jnp.float32)
        for d in (1, 3, 2):
            total = total + lax.ppermute(others[d - 1], "y", shift(4, d)).astype(jnp.float32)
        sums.append(total.astype(jnp.bfloat16))
    sums = [exchange_sum("zl", lambda i, v=v: columns(v, i * narrow, narrow)) for v in sums]
    return jnp.concatenate(sums, axis=0)


def join_cores(value):
    core = lax.axis_index("c")
    got = lax.ppermute(value, "c", SWAP)
    return jnp.where(core == 0, value, got), jnp.where(core == 0, got, value)


def dot(a, b, contract, precision=None):
    return lax.dot_general(
        a, b, (contract, ((), ())), precision=precision, preferred_element_type=jnp.float32
    )


def pack_kernel(table, core, total_ref, qt_ref, out_ref):
    def rows(index):
        return total_ref[pl.ds(pl.multiple_of(index * TILE, TILE), TILE), :]

    for k in range(SHARE):
        block = dot(rows(table[k, 0]), rows(table[k, 1]), ((1,), (1,)))
        out_ref[pl.ds(k, TILE, stride=SLOTS), :] = block
    half = ROWS // 2
    for b in range(half // TILE):
        part = dot(qt_ref[...], rows(core[0] * (half // TILE) + b), ((1,), (1,)))
        out_ref[pl.ds(b * RANK * SLOTS + SHARE, RANK, stride=SLOTS), :] = part


def pack(table, core, total, qt):
    return pl.pallas_call(
        pack_kernel,
        out_shape=jax.ShapeDtypeStruct((HOLDERS * SLOTS, TILE), jnp.float32),
        in_specs=[
            pl.BlockSpec(memory_space=pltpu.SMEM),
            pl.BlockSpec(memory_space=pltpu.SMEM),
            pl.BlockSpec(memory_space=pltpu.VMEM),
            pl.BlockSpec(memory_space=pltpu.VMEM),
        ],
        out_specs=pl.BlockSpec(memory_space=pltpu.VMEM),
        compiler_params=pltpu.CompilerParams(vmem_limit_bytes=4 * MIB),
    )(table, core, total, qt)


def small_kernel(body, rows, *args):
    vmem = pl.BlockSpec(memory_space=pltpu.VMEM)
    return pl.pallas_call(
        body,
        out_shape=jax.ShapeDtypeStruct((rows, TILE), jnp.float32),
        in_specs=[vmem],
        out_specs=vmem,
        compiler_params=pltpu.CompilerParams(vmem_limit_bytes=4 * MIB),
    )(*args)


def sum_kernel(parts_ref, out_ref):
    rows = RING_SIZE * SLOTS
    total = parts_ref[:rows, :]
    for p in range(1, parts_ref.shape[0] // rows):
        total = total + parts_ref[p * rows : (p + 1) * rows, :]
    for p in range(out_ref.shape[0] // rows):
        out_ref[p * rows : (p + 1) * rows, :] = total


def ring_kernel(parts_ref, out_ref):
    for k in range(SLOTS):
        row = jnp.sum(parts_ref[pl.ds(k, RING_SIZE, stride=SLOTS), :], axis=0, keepdims=True)
        out_ref[pl.ds(k, RING_SIZE, stride=SLOTS), :] = jnp.broadcast_to(row, (RING_SIZE, TILE))


def inverse_factor(gram):
    wide = (RANK, 2 * RANK)
    row = lax.broadcasted_iota(jnp.int32, wide, 0)
    lane = lax.broadcasted_iota(jnp.int32, wide, 1)
    eye = jnp.where(lane == row + RANK, 1.0, 0.0).astype(jnp.float32)
    work = jnp.concatenate([gram, eye[:, RANK:]], axis=1)
    result = jnp.zeros(wide, jnp.float32)
    for j in range(0, RANK, PIVOTS):
        rows = [work[j + a : j + a + 1, :] for a in range(PIVOTS)]
        cols = [jnp.broadcast_to(work[:, j + a : j + a + 1], wide) for a in range(PIVOTS)]
        corner = {
            (a, b): jnp.broadcast_to(work[j + a : j + a + 1, j + b : j + b + 1], (1, 2 * RANK))
            for a in range(PIVOTS)
            for b in range(a, PIVOTS)
        }
        for a in range(PIVOTS):
            inverse = 1.0 / corner[a, a]
            result = jnp.where(row == j + a, rows[a] * lax.rsqrt(corner[a, a]), result)
            for b in range(a + 1, PIVOTS):
                factor = corner[a, b] * inverse
                rows[b] = rows[b] - factor * rows[a]
                cols[b] = cols[b] - cols[a] * factor
                for c in range(b, PIVOTS):
                    corner[b, c] = corner[b, c] - factor * corner[a, c]
            cols[a] = cols[a] * inverse
        if j + PIVOTS < RANK:
            work = work - sum(cols[a] * rows[a] for a in range(PIVOTS))
    return result[:, RANK:]


def normal_kernel(left):
    gram = dot(left, left, ((1,), (1,)), lax.Precision.HIGHEST)
    inverse = inverse_factor(gram)
    return inverse, dot(inverse, left, ((1,), (0,)), lax.Precision.HIGHEST)


def iterate_kernel(core, own_table, other_table, own_ref, other_ref, total_ref, near_ref, across_ref, last_ref, spread_ref, high, low, left_ref):
    half = ROWS // 2
    high_scale = 1.0 / REPLICAS**2
    for table, blocks, place in ((own_table, own_ref, core[0]), (other_table, other_ref, 1 - core[0])):
        for k in range(SHARE):
            i = pl.ds(pl.multiple_of(table[k, 0] * TILE, TILE), TILE)
            j = pl.ds(pl.multiple_of(table[k, 1] * TILE, TILE), TILE)
            block = blocks[pl.ds(k, TILE, stride=SLOTS), :] * high_scale
            for at, value in (((i, j), block), ((j, i), block.T)):
                top = value.astype(jnp.bfloat16)
                high[at] = top
                low[at] = (value - top.astype(jnp.float32)).astype(jnp.bfloat16)
        for b in range(half // TILE):
            at = pl.ds(pl.multiple_of(place * half + b * TILE, TILE), TILE)
            left_ref[:, at] = blocks[pl.ds(b * RANK * SLOTS + SHARE, RANK, stride=SLOTS), :] / REPLICAS
    left = left_ref[...]
    for step in range(ITERS - 1):
        basis = normal_kernel(left)[1]
        pbt = basis.astype(jnp.bfloat16)
        left = dot(pbt, high[...], ((1,), (0,))) + dot(pbt, low[...], ((1,), (0,)))
    last_ref[...] = left
    left_ref[...] = left

    def product(part, columns_ref):
        return dot(part, columns_ref.astype(jnp.float32), ((1,), (0,)), lax.Precision.HIGHEST)

    spread_ref[0] = product(left, total_ref[...]) / REPLICAS
    halves = [left_ref[:, pl.ds(pl.multiple_of(side * half, half), half)] for side in (core[0], 1 - core[0])]
    for k in range(near_ref.shape[0]):
        spread_ref[k + 1] = (product(halves[0], near_ref[k]) + product(halves[1], across_ref[k])) / REPLICAS


def iterate(core, own_table, other_table, own, other, total, near, across):
    smem = pl.BlockSpec(memory_space=pltpu.SMEM)
    vmem = pl.BlockSpec(memory_space=pltpu.VMEM)
    return pl.pallas_call(
        iterate_kernel,
        out_shape=(
            jax.ShapeDtypeStruct((RANK, ROWS), jnp.float32),
            jax.ShapeDtypeStruct((4, RANK, TILE), jnp.float32),
        ),
        in_specs=[smem] * 3 + [vmem] * 5,
        out_specs=(vmem, vmem),
        scratch_shapes=[
            pltpu.VMEM((ROWS, ROWS), jnp.bfloat16),
            pltpu.VMEM((ROWS, ROWS), jnp.bfloat16),
            pltpu.VMEM((RANK, ROWS), jnp.float32),
        ],
        compiler_params=pltpu.CompilerParams(vmem_limit_bytes=14 * MIB),
    )(core, own_table, other_table, own, other, total, near, across)


def last_kernel(left_ref, inverse_ref, basis_ref):
    inverse_ref[...], basis_ref[...] = normal_kernel(left_ref[...])


def last_basis(left):
    vmem = pl.BlockSpec(memory_space=pltpu.VMEM)
    return pl.pallas_call(
        last_kernel,
        out_shape=(
            jax.ShapeDtypeStruct((RANK, RANK), jnp.float32),
            jax.ShapeDtypeStruct(left.shape, jnp.float32),
        ),
        in_specs=[vmem],
        out_specs=(vmem, vmem),
        compiler_params=pltpu.CompilerParams(vmem_limit_bytes=4 * MIB),
        cost_estimate=pl.CostEstimate(flops=1000, bytes_accessed=1000, transcendentals=0),
    )(left)


def corrected_kernel(grad_ref, error_ref, out_ref):
    value = grad_ref[...].astype(jnp.float32) + error_ref[...].astype(jnp.float32)
    out_ref[...] = value.astype(jnp.bfloat16)


def corrected_sum(grad, error):
    rows = pl.BlockSpec((2 * TILE, grad.shape[1]), lambda i: (i, 0))
    return pl.pallas_call(
        corrected_kernel,
        out_shape=jax.ShapeDtypeStruct(grad.shape, grad.dtype),
        grid=(ROWS // TILE // 2,),
        in_specs=[rows, rows],
        out_specs=rows,
        compiler_params=pltpu.CompilerParams(vmem_limit_bytes=60 * MIB),
        cost_estimate=pl.CostEstimate(flops=1000, bytes_accessed=1000, transcendentals=0),
    )(grad, error)


def finish_kernel(place, inverse_ref, *refs):
    *spread_refs, pbt_ref, corrected_ref, factor_ref, out_ref, wide, qbt, held, done = refs
    step = pl.program_id(0)
    rows = out_ref.shape[0]

    def fetch(k):
        at = pl.ds(pl.multiple_of(k * rows, rows), rows)
        return pltpu.make_async_copy(corrected_ref.at[at, :], held.at[k], done.at[k])

    @pl.when(step == 0)
    def _():
        for k in range(held.shape[0]):
            fetch(k).start()
        for d, spread_ref in enumerate(spread_refs):
            blocks, _, width = spread_ref.shape
            for k in range(blocks):
                block = lax.rem(place[0] + 4 - d, 4) * blocks + lax.rem(place[1] + blocks - k, blocks)
                wide[:, pl.ds(pl.multiple_of(block * width, width), width)] = spread_ref[k]
        right = dot(inverse_ref[...], wide[...], ((1,), (0,)), lax.Precision.HIGHEST)
        factor_ref[...] = right / math.sqrt(ROWS)
        qbt[...] = right.astype(jnp.bfloat16)

    approx = dot(pbt_ref[...], qbt[...], ((0,), (0,)))
    fetch(step).wait()
    out_ref[...] = (held[step].astype(jnp.float32) - approx).astype(jnp.bfloat16)


def finish(place, inverse, spreads, pbt, corrected):
    vmem = pl.BlockSpec(memory_space=pltpu.VMEM)
    cols = corrected.shape[1]
    rows = 2 * TILE
    return pl.pallas_call(
        finish_kernel,
        out_shape=(
            jax.ShapeDtypeStruct((RANK, cols), jnp.float32),
            jax.ShapeDtypeStruct((ROWS, cols), jnp.bfloat16),
        ),
        grid=(ROWS // rows,),
        in_specs=[pl.BlockSpec(memory_space=pltpu.SMEM), vmem]
        + [vmem] * len(spreads)
        + [pl.BlockSpec((RANK, rows), lambda i: (0, i)), pl.BlockSpec(memory_space=pl.ANY)],
        out_specs=(pl.BlockSpec((RANK, cols), lambda i: (0, 0)), pl.BlockSpec((rows, cols), lambda i: (i, 0))),
        scratch_shapes=[
            pltpu.VMEM((RANK, cols), jnp.float32),
            pltpu.VMEM((RANK, cols), jnp.bfloat16),
            pltpu.VMEM((ROWS // rows, rows, cols), jnp.bfloat16),
            pltpu.SemaphoreType.DMA((ROWS // rows,)),
        ],
        compiler_params=pltpu.CompilerParams(vmem_limit_bytes=60 * MIB),
    )(place, inverse, *spreads, pbt, corrected)


def sum_chips(value, later):
    rows = RING_SIZE * SLOTS

    def swap(v, axes, size):
        v = lax.all_to_all(v.reshape(size, rows, TILE), axes, 0, 0, tiled=True)
        return v.reshape(size * rows, TILE)

    def ring(v):
        v = lax.all_to_all(v.reshape(RING_SIZE, SLOTS, 1, TILE), RING, 0, 0, tiled=True)
        return v.reshape(rows, TILE)

    part = small_kernel(sum_kernel, rows, swap(value, PLANE, PLANE_SIZE))
    part = ring(small_kernel(ring_kernel, rows, ring(part)))
    part, later = lax.optimization_barrier((part, later))
    return swap(small_kernel(sum_kernel, PLANE_SIZE * rows, part), PLANE, PLANE_SIZE), later


def shards(grad, error, q_init):
    core, y, zl = (lax.axis_index(a) for a in ("c", "y", "zl"))
    mine = reduce_replicas(grad[0], error[0])
    width = mine.shape[1]
    total = jnp.concatenate(join_cores(mine), axis=0)
    qt = lax.dynamic_slice(q_init, ((y * 4 + zl) * width, 0), (width, RANK)).T
    table = jnp.asarray(TABLE)
    own_table = lax.dynamic_index_in_dim(table, core, 0, False)
    other_table = lax.dynamic_index_in_dim(table, 1 - core, 0, False)
    which = core.reshape(1)
    packed = pack(own_table, which, total, qt)
    grad, error, packed = lax.optimization_barrier((grad, error, packed))
    corrected = corrected_sum(grad[0], error[0])
    own, mine = sum_chips(packed, mine)
    near = {d: lax.ppermute(mine, "zl", shift(4, d)) for d in (1, 3, 2)}
    near = jnp.stack([near[1], near[2], near[3]])
    own, corrected, near = lax.optimization_barrier((own, corrected, near))
    across = lax.ppermute(near, "c", SWAP)
    other = lax.ppermute(own, "c", SWAP)
    left, spread = iterate(which, own_table, other_table, own, other, total, near, across)
    spreads = {d: lax.ppermute(spread, "y", shift(4, d)) for d in (1, 3, 2)}
    spreads = [spread, spreads[1], spreads[2], spreads[3]]
    inverse, basis = last_basis(left)
    factor, new_error = finish(jnp.stack([y, zl]), inverse, spreads, basis.astype(jnp.bfloat16), corrected)
    own_rows = ROWS // 256
    start = lax.axis_index(("zl", "y", "c", "x", "zh")) * own_rows
    own_basis = lax.dynamic_slice(basis, (0, start), (RANK, own_rows)).T
    return (own_basis * math.sqrt(ROWS), factor.T, new_error[None])


def solution(mesh):
    fine = Mesh(mesh.devices.reshape(4, 4, 2, 4, 2), ("zl", "y", "c", "x", "zh"))
    dp, tensor = ("zl", "y", "c"), ("x", "zh")
    placed = (P(dp, None, tensor), P(dp, None, tensor), P(tensor, None))
    return jax.shard_map(
        shards,
        mesh=fine,
        in_specs=placed,
        out_specs=(P(dp + tensor, None), P(tensor, None), P(dp, None, tensor)),
        check_vma=False,
    )
```
